32 devices in a mesh: dp: 4 (over y, core), ctx: 4 (over z), fsdp: 2 (over x).
Axes of the slice: x: 2, y: 2, z: 4, core: 2. Of those that a mesh axis runs over, the one named last changes fastest.
Arguments:
- tokens: bfloat16 [8, 1024, 2048], P(('dp', 'fsdp'), 'ctx'), may hold values from -6 to 6
- cotangent: bfloat16 [8, 1024, 2048], P(('dp', 'fsdp'), 'ctx'), may hold values from -6 to 6
- norm1_gain: float32 [2048], P('fsdp'), may hold values from 0.5 to 1.5
- norm1_bias: float32 [2048], P('fsdp'), may hold values from -1.5 to 1.5
- norm2_gain: float32 [2048], P('fsdp'), may hold values from 0.5 to 1.5
- norm2_bias: float32 [2048], P('fsdp'), may hold values from -1.5 to 1.5
- w_query: bfloat16 [2048, 2048], P('fsdp'), may hold values from -0.125 to 0.125
- w_key: bfloat16 [2048, 2048], P('fsdp'), may hold values from -0.125 to 0.125
- w_value: bfloat16 [2048, 2048], P('fsdp'), may hold values from -0.125 to 0.125
- b_query: float32 [2048], P('fsdp'), may hold values from -1.5 to 1.5
- b_key: float32 [512], P('fsdp'), may hold values from -1.5 to 1.5
- b_value: float32 [2048], P('fsdp'), may hold values from -1.5 to 1.5
- w_out: bfloat16 [2048, 2048], P('fsdp'), may hold values from -0.5 to 0.5
- b_out: float32 [2048], P('fsdp'), may hold values from -1.5 to 1.5
- w_up: bfloat16 [2048, 8192], P('fsdp'), may hold values from -0.125 to 0.125
- b_up: float32 [8192], P('fsdp'), may hold values from -1.5 to 1.5
- w_down: bfloat16 [2048, 8192], P('fsdp'), may hold values from -0.0625 to 0.0625
- b_down: float32 [2048], P('fsdp'), may hold values from -1.5 to 1.5
Outputs:
- mixed: bfloat16 [8, 1024, 2048], P(('dp', 'fsdp'), 'ctx')
- grad_tokens: float32 [8, 1024, 2048], P(('dp', 'fsdp'), 'ctx')
- grad_norm1_gain: float32 [2048], P('fsdp')
- grad_norm1_bias: float32 [2048], P('fsdp')
- grad_norm2_gain: float32 [2048], P('fsdp')
- grad_norm2_bias: float32 [2048], P('fsdp')
- grad_w_query: float32 [2048, 2048], P('fsdp')
- grad_w_key: float32 [2048, 2048], P('fsdp')
- grad_w_value: float32 [2048, 2048], P('fsdp')
- grad_b_query: float32 [2048], P('fsdp')
- grad_b_key: float32 [512], P('fsdp')
- grad_b_value: float32 [2048], P('fsdp')
- grad_w_out: float32 [2048, 2048], P('fsdp')
- grad_b_out: float32 [2048], P('fsdp')
- grad_w_up: float32 [2048, 8192], P('fsdp')
- grad_b_up: float32 [8192], P('fsdp')
- grad_w_down: float32 [2048, 8192], P('fsdp')
- grad_b_down: float32 [2048], P('fsdp')
The draws below stay inside these ranges and needn't reach their ends.
All inputs are finite; a program needn't handle non-finite values.
Results may differ from the reference program's by a relative error of at most 0.025.
Values may be sent and summed in bfloat16 or wider, within the bound.
No kernel may reach another device: no remote copies, remote signals or barrier semaphores. Data moves between devices by JAX's collectives and lax.ppermute only.
A program may use at most 768 MiB of HBM per device.

```python
import math
import jax
import jax.numpy as jnp
from jax import lax

D = 2048
HEAD_DIM = 256
ROT = 64
FF = 8192
HEADS = 8
LENGTH = 1024
SEQS = 8


def block_scale(stream_key, dims, split, smallest, top_value):
    gain, own = 1.0, jax.random.fold_in(stream_key, 6)
    for dim, shards_of in split:
        draws = jnp.exp(jax.random.uniform(jax.random.fold_in(own, dim), (shards_of,), jnp.float32, smallest / len(split), top_value / len(split)))
        gain = gain * jnp.repeat(draws, dims[dim] // shards_of).reshape([-1 if axis == dim else 1 for axis in range(len(dims))])
    return gain


def bell_draw(stream_key, dims, width, most, split=(), held_as=jnp.bfloat16):
    result = jax.random.normal(stream_key, dims, jnp.float32) * width
    if len(split) > 0:
        result = block_scale(stream_key, dims, split, -0.22, 0.18) * result
    return jnp.clip(result, min=-most, max=most).astype(held_as)


def setup_inputs(seed: int = 0) -> dict:
    splits = jax.random.split(jax.random.key(seed), 19)
    return {
        "tokens": bell_draw(splits[0], (SEQS, LENGTH, D), 1.0, 6.0, ((0, 8), (1, 4))),
        "cotangent": bell_draw(splits[1], (SEQS, LENGTH, D), 1.0, 6.0, ((0, 8), (1, 4))),
        "norm1_gain": jnp.clip(1.0 + 0.1 * jax.random.normal(splits[2], (D,), jnp.float32), 0.5, 1.5),
        "norm1_bias": bell_draw(splits[3], (D,), 0.3, 1.5, ((0, 2),), jnp.float32),
        "norm2_gain": jnp.clip(1.0 + 0.1 * jax.random.normal(splits[4], (D,), jnp.float32), 0.5, 1.5),
        "norm2_bias": bell_draw(splits[5], (D,), 0.3, 1.5, ((0, 2),), jnp.float32),
        "w_query": bell_draw(splits[6], (D, D), D ** -0.5, 0.125, ((0, 2),)),
        "w_key": bell_draw(splits[7], (D, D), D ** -0.5, 0.125, ((0, 2),)),
        "w_value": bell_draw(splits[8], (D, D), D ** -0.5, 0.125, ((0, 2),)),
        "b_query": bell_draw(splits[9], (D,), 0.3, 1.5, ((0, 2),), jnp.float32),
        "b_key": bell_draw(splits[10], (HEADS * ROT,), 0.3, 1.5, ((0, 2),), jnp.float32),
        "b_value": bell_draw(splits[11], (D,), 0.3, 1.5, ((0, 2),), jnp.float32),
        "w_out": bell_draw(splits[12], (D, D), (D // 16) ** -0.5, 0.5, ((0, 2),)),
        "b_out": bell_draw(splits[13], (D,), 0.3, 1.5, ((0, 2),), jnp.float32),
        "w_up": bell_draw(splits[14], (D, FF), D ** -0.5, 0.125, ((0, 2),)),
        "b_up": bell_draw(splits[15], (FF,), 0.3, 1.5, ((0, 2),), jnp.float32),
        "w_down": bell_draw(splits[16], (D, FF), FF ** -0.5, 0.0625, ((0, 2),)),
        "b_down": bell_draw(splits[17], (D,), 0.3, 1.5, ((0, 2),), jnp.float32),
    }


@jax.custom_vjp
def low(v):
    return lax.optimization_barrier(v.astype(jnp.bfloat16)).astype(jnp.float32)

@jax.custom_vjp
def low_back(v):
    return v

def low_keep(v):
    return (low(v), None)

def low_pass(kept, grad):
    return (grad,)

def back_keep(v):
    return (v, None)

def back_low(kept, grad):
    return (low(grad),)
low.defvjp(low_keep, low_pass)
low_back.defvjp(back_keep, back_low)
norm_eps = 1e-05
masked_score = -1e+30

def highest(left, right):
    return jnp.dot(left, right, precision=lax.Precision.HIGHEST, preferred_element_type=jnp.float32)

def layer_norm(values, gain_vec, shift_vec):
    center = values - lax.optimization_barrier(jnp.mean(values, axis=-1, keepdims=True))
    spread = lax.optimization_barrier(jnp.mean(center * center, axis=-1, keepdims=True))
    return center * lax.rsqrt(spread + norm_eps) * gain_vec + shift_vec

def angle_tables(position):
    half_rot = ROT // 2
    inverse = 10000.0 ** (-2.0 * jnp.arange(half_rot, dtype=jnp.float32) / ROT)
    angles = position.astype(jnp.float32)[:, None] * inverse[None, :]
    return (jnp.cos(angles), jnp.sin(angles))

def rotate(values, cosine, sine_part):
    half_rot = ROT // 2
    first_half = values[..., :half_rot]
    second_half = values[..., half_rot:ROT]
    cos_wide = cosine[:, None, :]
    sin_wide = sine_part[:, None, :]
    return jnp.concatenate([first_half * cos_wide - second_half * sin_wide, second_half * cos_wide + first_half * sin_wide, values[..., ROT:]], axis=-1)

def attend_block(query_blk, row_start, key_heads, value_heads):
    seq_len = key_heads.shape[0]
    query_rows = query_blk.shape[0]
    scores = jnp.einsum('qhd,khd->hqk', query_blk, key_heads, precision=lax.Precision.HIGHEST) / math.sqrt(HEAD_DIM)
    scores = low_back(scores)
    query_pos = row_start + jnp.arange(query_rows, dtype=jnp.int32)
    key_pos = jnp.arange(seq_len, dtype=jnp.int32)
    allowed = (key_pos[None, :] <= query_pos[:, None])[None]
    top_score = lax.optimization_barrier(jnp.max(jnp.where(allowed, scores, masked_score), axis=-1))
    exp_terms = jnp.where(allowed, jnp.exp(scores - top_score[..., None]), 0.0)
    row_total = lax.optimization_barrier(jnp.sum(exp_terms, axis=-1))
    summed = jnp.einsum('hqk,khd->qhd', low(exp_terms), value_heads, precision=lax.Precision.HIGHEST)
    return summed / jnp.transpose(row_total)[:, :, None]

def forward(seq_tokens, parameters):
    norm1_gain, norm1_bias, norm2_gain, norm2_bias, w_query, w_key, w_value, b_query, b_key, b_value, w_out, b_out, w_up, b_up, w_down, b_down = parameters
    seq_len = seq_tokens.shape[0]
    head_count = D // HEAD_DIM
    first_in = low(layer_norm(seq_tokens, norm1_gain, norm1_bias))
    second_in = low(layer_norm(seq_tokens, norm2_gain, norm2_bias))
    key_shift = jnp.pad(b_key.reshape(head_count, ROT), ((0, 0), (0, HEAD_DIM - ROT))).reshape(D)
    query_lin = low_back(highest(first_in, w_query) + b_query)
    key_lin = low_back(highest(first_in, w_key) + key_shift)
    value_lin = low_back(highest(first_in, w_value) + b_value)
    cosine, sine_part = angle_tables(jnp.arange(seq_len, dtype=jnp.int32))
    query_rot = low(rotate(query_lin.reshape(seq_len, head_count, HEAD_DIM), cosine, sine_part))
    key_rot = low(rotate(key_lin.reshape(seq_len, head_count, HEAD_DIM), cosine, sine_part))
    value_low = low(value_lin.reshape(seq_len, head_count, HEAD_DIM))
    block_rows = math.gcd(seq_len, 512)
    block_count = seq_len // block_rows
    attend = jax.checkpoint(attend_block)

    def one_block(packed):
        return attend(packed[0], packed[1], key_rot, value_low)
    mapped = lax.map(one_block, (query_rot.reshape(block_count, block_rows, head_count, HEAD_DIM), jnp.arange(block_count, dtype=jnp.int32) * block_rows))
    attended = low(low_back(mapped.reshape(seq_len, D)))
    hidden_pre = low_back(highest(second_in, w_up) + b_up)
    activated = low(jax.nn.gelu(hidden_pre, approximate=False))
    return seq_tokens + highest(attended, w_out.T) + b_out + highest(activated, w_down.T) + b_down

def reference(tokens, cotangent, norm1_gain, norm1_bias, norm2_gain, norm2_bias, w_query, w_key, w_value, b_query, b_key, b_value, w_out, b_out, w_up, b_up, w_down, b_down):
    parameters = tuple((member.astype(jnp.float32) for member in (norm1_gain, norm1_bias, norm2_gain, norm2_bias, w_query, w_key, w_value, b_query, b_key, b_value, w_out, b_out, w_up, b_up, w_down, b_down)))

    def one_seq(totals, packed):
        seq_in, seq_cot = packed
        mixed_out, pull_back = jax.vjp(forward, seq_in.astype(jnp.float32), parameters)
        grad_in, grad_params = pull_back(seq_cot.astype(jnp.float32))
        totals = jax.tree.map(jnp.add, totals, grad_params)
        return (totals, (mixed_out.astype(jnp.bfloat16), grad_in))
    zeros_init = tuple((jnp.zeros_like(member) for member in parameters))
    totals, (mixed, grad_tokens) = lax.scan(one_seq, zeros_init, (tokens, cotangent))
    return (mixed, grad_tokens, totals[0], totals[1], totals[2], totals[3], totals[4], totals[5], totals[6], totals[7], totals[8], totals[9], totals[10], totals[11], totals[12], totals[13], totals[14], totals[15])
```

```python
import functools
import math

import jax
import jax.numpy as jnp
from jax import lax
from jax.experimental import pallas as pl
from jax.experimental.pallas import tpu as pltpu
from jax.sharding import PartitionSpec as P

HEAD_DIM = 256
ROT = 64
HALF = ROT // 2
LANES = 128
CORES = 2
norm_eps = 1e-05
masked_score = -1e30
MIB = 1 << 20
f32 = jnp.float32
bf16 = jnp.bfloat16
SCALE = 1.0 / math.sqrt(HEAD_DIM)
F_AT, J_AT, Y_AT, Z_AT, C_AT = range(5)


def dot(left, right, dims):
    return lax.dot_general(left, right, (dims, ((), ())), preferred_element_type=f32)


def mm(left, right):
    return dot(left, right, ((1,), (0,)))


def mm_rows(left, right):
    return dot(left, right, ((1,), (1,)))


def mm_tokens(left, right):
    return dot(left, right, ((0,), (0,)))


def array(shape, dtype):
    return jax.ShapeDtypeStruct(shape, dtype)


ANY = pl.BlockSpec(memory_space=pl.ANY)
PLANNED = {
    "join": 2,
    "forward": 18,
    "attend": 2,
    "branch": 10,
    "sum_mixed": 4,
    "down_back": 10,
    "grad_down": 9,
    "grad_up": 9,
    "grad_att": 9,
    "attend_back": 6,
    "back": 13,
    "sum_back": 4,
    "sum_fsdp": 2,
    "sum_pairs": 8,
    "sum_small": 1,
    "pin": 15,
    "place": 4,
    "mixed": 3,
    "grad_tokens": 4,
}


class Chain:
    def __init__(self, at):
        self.at = at
        self.last = None

    def __call__(self, kernel, outs, grid, in_specs, out_specs, operands, aliases=None, scratch=(), name=None, limit=50, after=()):
        n_in, n_out = len(operands), len(outs)
        extra = ([] if self.last is None else [self.last]) + list(after)

        def body(at_ref, *refs):
            ins = refs[:n_in]
            made = refs[n_in + len(extra) :]
            kernel(at_ref, ins, made[:n_out], made[n_out + 1 :])

        result = pl.pallas_call(
            body,
            out_shape=tuple(outs) + (array((8, LANES), f32),),
            grid_spec=pltpu.PrefetchScalarGridSpec(
                num_scalar_prefetch=1,
                grid=grid,
                in_specs=list(in_specs) + [ANY] * len(extra),
                out_specs=list(out_specs) + [ANY],
                scratch_shapes=list(scratch),
            ),
            input_output_aliases=aliases or {},
            compiler_params=pltpu.CompilerParams(vmem_limit_bytes=limit * MIB),
            cost_estimate=pl.CostEstimate(
                flops=int(1.15e4 * PLANNED[name]), bytes_accessed=1, transcendentals=0
            ),
            name=name,
        )(self.at, *operands, *extra)
        self.last = result[-1]
        return result[:-1]


def rem(a, n):
    return lax.rem(a, jnp.int32(n))


def columns(at_ref, k, n_f, rows):
    block = rem(at_ref[F_AT] + n_f - k, n_f)
    return pl.ds(pl.multiple_of(block * rows, rows), rows)


def turn(v, cos_t, sin_a, sin_b):
    low = v[:, :LANES]
    low = low * cos_t + pltpu.roll(low, LANES - HALF, 1) * sin_a + pltpu.roll(low, HALF, 1) * sin_b
    return jnp.concatenate([low, v[:, LANES:]], axis=1)


def shift_perm(count, step):
    return [(i, (i + step) % count) for i in range(count)]


def local(
    n_dp,
    n_ctx,
    n_f,
    tokens,
    cotangent,
    norm1_gain,
    norm1_bias,
    norm2_gain,
    norm2_bias,
    w_query,
    w_key,
    w_value,
    b_query,
    b_key,
    b_value,
    w_out,
    b_out,
    w_up,
    b_up,
    w_down,
    b_down,
):
    n_y = n_dp // CORES
    dp_idx, z_idx, f_idx = lax.axis_index("dp"), lax.axis_index("ctx"), lax.axis_index("fsdp")
    y_idx, c_idx = dp_idx // CORES, dp_idx % CORES
    splits = n_ctx * CORES
    j_idx = z_idx * CORES + c_idx
    block_rows, width = tokens.shape[1], tokens.shape[2]
    length = block_rows * n_ctx
    hidden = w_up.shape[1]
    heads = width // HEAD_DIM
    rows = width // n_f
    n_att, n_hid = width // splits, hidden // splits
    assert n_att == HEAD_DIM and n_ctx == 4
    n_qkv = 3 * n_att
    half_hid = n_hid // 2
    at = jnp.stack([f_idx, j_idx, y_idx, z_idx, c_idx]).astype(jnp.int32)
    run = Chain(at)

    def core_swap(value):
        return lax.ppermute(value, "dp", [(i, i ^ 1) for i in range(n_dp)])

    def over_y(value, step):
        return lax.ppermute(value, "dp", shift_perm(n_dp, CORES * step))

    def over_z(value, step):
        return lax.ppermute(value, "ctx", shift_perm(n_ctx, step))

    def over_f(value, step):
        return lax.ppermute(value, "fsdp", shift_perm(n_f, step))

    def mine(w, n):
        return lax.dynamic_slice_in_dim(w, j_idx * n, n, axis=1)

    small = [norm1_gain, norm1_bias, norm2_gain, norm2_bias, b_query, b_key, b_value, b_out + b_down, b_up]
    sizes = [s.shape[0] for s in small]
    ends = [sum(sizes[:i]) for i in range(len(sizes) + 1)]
    small_own = jnp.concatenate(small)
    small_got = [small_own] + [over_f(small_own, k) for k in range(1, n_f)]

    own_tok = lax.all_gather(tokens[0], "ctx", axis=0, tiled=True)
    own_cot = lax.all_gather(cotangent[0], "ctx", axis=0, tiled=True)
    cot = (own_cot, core_swap(own_cot))

    def pin(value, after=()):
        return run(lambda *a: None, [array(value.shape, value.dtype)], (1,), [ANY], [ANY], [value], aliases={1: 0}, name="pin", limit=4, after=after)[0]

    def fetch(part):
        return [over_f(part, k) for k in range(1, n_f)]

    y_part = rows // n_y
    got_u = fetch(lax.dynamic_slice(w_up, (y_idx * y_part, j_idx * n_hid), (y_part, n_hid)))
    got_qkv = fetch(jnp.concatenate([mine(w_query, n_att), mine(w_key, n_att), mine(w_value, n_att)], axis=1))
    got_do = fetch(jnp.concatenate([mine(w_down, n_hid), mine(w_out, n_att)], axis=1))

    def whole(i):
        pieces = [g[ends[i] : ends[i + 1]] for g in small_got]
        if n_f == 2:
            return jnp.concatenate([jnp.where(f_idx == m, pieces[0], pieces[1]) for m in range(2)])
        rolled = jnp.stack(pieces[::-1])
        return jnp.roll(rolled, f_idx + 1, axis=0).reshape(-1)

    gain1, shift1, gain2, shift2, bq, bk, bv, b_last, bu = [whole(i) for i in range(len(small))]

    def part(vec, n):
        return lax.dynamic_slice_in_dim(vec, j_idx * n, n, axis=0)

    def eight(vec):
        return jnp.broadcast_to(vec[None], (8, vec.shape[0]))

    vecs = jnp.concatenate([jnp.stack([gain1, shift1, gain2, shift2]), jnp.zeros((4, width), f32)])
    key_shift = jnp.pad(part(bk, ROT), (0, HEAD_DIM - ROT))
    bias_qkv = eight(jnp.concatenate([part(bq, n_att), key_shift, part(bv, n_att)]))
    bias_up = eight(part(bu, n_hid))
    bias_last = eight(b_last)
    positions = jnp.arange(length, dtype=f32)
    inverse = 10000.0 ** (-2.0 * jnp.arange(HALF, dtype=f32) / ROT)
    angles = positions[:, None] * inverse[None, :]
    cosine, sine = jnp.cos(angles), jnp.sin(angles)
    none = jnp.zeros((length, LANES - ROT), f32)
    zero = jnp.zeros_like(sine)
    tables = (
        jnp.concatenate([cosine, cosine, none + 1.0], axis=1),
        jnp.concatenate([-sine, zero, none], axis=1),
        jnp.concatenate([zero, sine, none], axis=1),
    )

    def join_kernel(at_ref, ins, outs, scratch):
        for k, r in enumerate(ins):

            @pl.when(pl.program_id(0) == k)
            def _(r=r):
                outs[0][0] = r[...]

    def share(piece):
        piece = pin(piece)
        parts = [piece] + [over_y(piece, k) for k in range(1, n_y)]
        joined = run(
            join_kernel,
            [array((n_y, y_part, n_hid), bf16)],
            (n_y,),
            [pl.BlockSpec((y_part, n_hid), lambda i, at: (0, 0))] * n_y,
            [pl.BlockSpec((1, y_part, n_hid), lambda i, at: (rem(at[Y_AT] + n_y - i, n_y), 0, 0))],
            parts,
            name="join",
            limit=16,
        )[0]
        return joined.reshape(rows, n_hid)

    vecs, bias_qkv, bias_up = pin(vecs), pin(bias_qkv), pin(bias_up)
    tables = tuple(pin(t) for t in tables)
    got_u = [share(g) for g in got_u]
    own_tok = pin(own_tok)
    tok = ([own_tok], [core_swap(own_tok[m * block_rows : (m + 1) * block_rows]) for m in range(n_ctx)])

    def rows_of(n, w):
        return pl.BlockSpec((n, w), lambda i, at: (i, 0))

    def fixed(n, w):
        return pl.BlockSpec((n, w), lambda i, at: (0, 0))

    def column(n, w):
        return pl.BlockSpec((n, w), lambda i, at: (0, at[J_AT]))

    own_qkv = [w_query, w_key, w_value]
    qkv_specs = [column(rows, n_att)] * 3 + [fixed(rows, n_qkv)] * (n_f - 1)
    u_specs = [column(rows, n_hid)] + [fixed(rows, n_hid)] * (n_f - 1)
    do_specs = [column(rows, n_hid), column(rows, n_att)] + [fixed(rows, n_hid + n_att)] * (n_f - 1)
    step = min(256, length)
    tok_grid = (length // step,)
    n_vec = len(tables)

    def forward_kernel(n_x, at_ref, ins, outs, scratch):
        x_refs, ins = ins[:n_x], ins[n_x:]
        vec_ref, cos_ref, sa_ref, sb_ref, bqkv_ref, bu_ref = ins[:6]
        wu = ins[6 : 6 + n_f]
        wq, wk, wv = ins[6 + n_f : 9 + n_f]
        w_other = ins[9 + n_f :]
        a1_ref, a2_ref, act_ref, slope_ref, qkv_ref = outs

        def normalize(x_ref):
            x = x_ref[...].astype(f32)
            center = x - jnp.mean(x, axis=-1, keepdims=True)
            spread = jnp.mean(center * center, axis=-1, keepdims=True)
            n = center * lax.rsqrt(spread + norm_eps)
            a1_ref[...] = (n * vec_ref[0:1] + vec_ref[1:2]).astype(bf16)
            a2_ref[...] = (n * vec_ref[2:3] + vec_ref[3:4]).astype(bf16)

        each = length // step // n_x
        for m, x_ref in enumerate(x_refs):
            if n_x == 1:
                normalize(x_ref)
            else:
                pl.when(pl.program_id(0) // each == m)(functools.partial(normalize, x_ref))
        h = jnp.broadcast_to(bu_ref[0:1], (step, n_hid))
        for k in range(n_f):
            h = h + mm(a2_ref[:, columns(at_ref, k, n_f, rows)], wu[k][...])
        cdf = 0.5 * (1.0 + lax.erf(h * (1.0 / math.sqrt(2.0))))
        pdf = jnp.exp(-0.5 * h * h) * (1.0 / math.sqrt(2.0 * math.pi))
        act_ref[...] = (h * cdf).astype(bf16)
        slope_ref[...] = (cdf + h * pdf).astype(bf16)
        cos_t, sa, sb = cos_ref[...], sa_ref[...], sb_ref[...]
        for m, w_own in enumerate((wq, wk, wv)):
            lanes = slice(m * n_att, (m + 1) * n_att)
            v = mm(a1_ref[:, columns(at_ref, 0, n_f, rows)], w_own[...]) + bqkv_ref[0:1, lanes]
            for k in range(1, n_f):
                v = v + mm(a1_ref[:, columns(at_ref, k, n_f, rows)], w_other[k - 1][:, lanes])
            qkv_ref[:, lanes] = (turn(v, cos_t, sa, sb) if m < 2 else v).astype(bf16)

    def forward(xs):
        each = length // step // len(xs)

        def rows_in(m):
            return pl.BlockSpec((step, width), lambda i, at: (jnp.clip(i - m * each, 0, each - 1), 0))

        return run(
            functools.partial(forward_kernel, len(xs)),
            [array((length, width), bf16)] * 2 + [array((length, n_hid), bf16)] * 2 + [array((length, n_qkv), bf16)],
            tok_grid,
            [rows_in(m) for m in range(len(xs))]
            + [fixed(8, width)]
            + [rows_of(step, LANES)] * n_vec
            + [fixed(8, n_qkv), fixed(8, n_hid)]
            + u_specs
            + qkv_specs,
            [rows_of(step, width)] * 2 + [rows_of(step, n_hid)] * 2 + [rows_of(step, n_qkv)],
            [*xs, vecs, *tables, bias_qkv, bias_up, w_up, *got_u, *own_qkv, *got_qkv],
            name="forward",
        )

    q_block = min(256, length)

    def masked(lo, hi):
        rows_at = lo + lax.broadcasted_iota(jnp.int32, (hi - lo, hi), 0)
        return lax.broadcasted_iota(jnp.int32, (hi - lo, hi), 1) <= rows_at

    def attend_kernel(at_ref, ins, outs, scratch):
        (qkv_ref,) = ins
        att_ref, lse_ref = outs
        for lo in range(0, length, q_block):
            hi = lo + q_block
            s = mm_rows(qkv_ref[lo:hi, :n_att], qkv_ref[:hi, n_att : 2 * n_att]) * SCALE
            allowed = masked(lo, hi)
            s = jnp.where(allowed, s, masked_score)
            top = jnp.max(s, axis=-1, keepdims=True)
            e = jnp.where(allowed, jnp.exp(s - top), 0.0)
            total = jnp.sum(e, axis=-1, keepdims=True)
            att_ref[lo:hi] = (mm(e.astype(bf16), qkv_ref[:hi, 2 * n_att :]) / total).astype(bf16)
            lse_ref[lo:hi] = jnp.broadcast_to(top + jnp.log(total), (q_block, LANES))

    def attend(qkv):
        return run(
            attend_kernel,
            [array((length, n_att), bf16), array((length, LANES), f32)],
            (1,),
            [fixed(length, n_qkv)],
            [fixed(length, n_att), fixed(length, LANES)],
            [qkv],
            name="attend",
        )

    def attend_back_kernel(at_ref, ins, outs, scratch):
        qkv_ref, do_ref, lse_ref, cos_ref, sa_ref, sb_ref = ins
        grad_ref, sum_ref = outs
        dk_acc, dv_acc = scratch
        q_sum = jnp.zeros((1, n_att), f32)
        for lo in range(0, length, q_block):
            hi = lo + q_block
            qi, ki, vi = qkv_ref[lo:hi, :n_att], qkv_ref[:hi, n_att : 2 * n_att], qkv_ref[:hi, 2 * n_att :]
            do = do_ref[lo:hi]
            s = mm_rows(qi, ki) * SCALE
            chance = jnp.where(masked(lo, hi), jnp.exp(s - lse_ref[lo:hi, 0:1]), 0.0)
            d_chance = mm_rows(do, vi)
            row_dot = jnp.sum(chance * d_chance, axis=-1, keepdims=True)
            ds = (chance * (d_chance - row_dot)).astype(bf16)
            dq = turn(mm(ds, ki) * SCALE, cos_ref[lo:hi], -sa_ref[lo:hi], -sb_ref[lo:hi]).astype(bf16)
            grad_ref[lo:hi, :n_att] = dq
            q_sum = q_sum + jnp.sum(dq.astype(f32), axis=0, keepdims=True)
            dk, dv = mm_tokens(ds, qi), mm_tokens(chance.astype(bf16), do)
            if lo > 0:
                dk_acc[:lo] += dk[:lo]
                dv_acc[:lo] += dv[:lo]
            dk_acc[lo:hi] = dk[lo:]
            dv_acc[lo:hi] = dv[lo:]
        dk = turn(dk_acc[...] * SCALE, cos_ref[...], -sa_ref[...], -sb_ref[...]).astype(bf16)
        dv = dv_acc[...].astype(bf16)
        grad_ref[:, n_att : 2 * n_att] = dk
        grad_ref[:, 2 * n_att :] = dv
        sums = (q_sum, jnp.sum(dk.astype(f32), axis=0, keepdims=True), jnp.sum(dv.astype(f32), axis=0, keepdims=True))
        for m, total in enumerate(sums):
            sum_ref[:, m * n_att : (m + 1) * n_att] = jnp.broadcast_to(total, (8, n_att))

    def attend_back(qkv, do, lse):
        return run(
            attend_back_kernel,
            [array((length, n_qkv), bf16), array((8, n_qkv), f32)],
            (1,),
            [fixed(length, n_qkv), fixed(length, n_att)] + [fixed(length, LANES)] * (1 + n_vec),
            [fixed(length, n_qkv), fixed(8, n_qkv)],
            [qkv, do, lse, *tables],
            scratch=[pltpu.VMEM((length, n_att), f32)] * 2,
            name="attend_back",
        )

    def down_out(refs, k):
        if k == 0:
            return refs[0][...], refs[1][...]
        return refs[1 + k][:, :n_hid], refs[1 + k][:, n_hid:]

    def branch_kernel(at_ref, ins, outs, scratch):
        act_ref, att_ref = ins[:2]
        for k in range(n_f):
            wd, wo = down_out(ins[2:], k)
            value = mm_rows(act_ref[...], wd) + mm_rows(att_ref[...], wo)
            outs[0][:, columns(at_ref, k, n_f, rows)] = value.astype(bf16)

    def branch(act, att):
        return run(
            branch_kernel,
            [array((length, width), bf16)],
            tok_grid,
            [rows_of(step, n_hid), rows_of(step, n_att)] + do_specs,
            [rows_of(step, width)],
            [act, att, w_down, w_out, *got_do],
            name="branch",
        )[0]

    def split_kernel(count, at_ref, ins, outs, scratch):
        for k in range(count):

            @pl.when(pl.program_id(0) == k)
            def _(k=k):
                total = ins[0][...].astype(f32)
                for r in ins[1:]:
                    total = total + r[...].astype(f32)
                outs[k][...] = total.astype(outs[k].dtype)

    def split_sum(values, count, where, name):
        n, w = values[0].shape
        spec = pl.BlockSpec((n // count, w), lambda i, at: (i if where is None else rem(at[where] + i, count), 0))
        return run(
            functools.partial(split_kernel, count),
            [array((n // count, w), f32 if k == 0 else bf16) for k in range(count)],
            (count,),
            [spec] * len(values),
            [fixed(n // count, w)] * count,
            values,
            name=name,
            limit=16,
        )

    def add_kernel(at_ref, ins, outs, scratch):
        total = ins[0][...].astype(f32)
        for r in ins[1:]:
            total = total + r[...].astype(f32)
        outs[0][...] = total.astype(outs[0].dtype)

    def add(values, dtype, name):
        n, w = values[0].shape
        m = n // 2 if n % 32 == 0 else n
        return run(
            add_kernel,
            [array((n, w), dtype)],
            (n // m,),
            [rows_of(m, w)] * len(values),
            [rows_of(m, w)],
            values,
            name=name,
            limit=16,
        )[0]

    def to_owners(own, other_got, name):
        return lax.psum_scatter(add([own, other_got], bf16, name), "ctx", scatter_dimension=0, tiled=True)

    def down_back_kernel(at_ref, ins, outs, scratch):
        c_ref, slope_ref = ins[:2]
        pre_ref, do_ref, sum_ref = outs
        g_act = jnp.zeros((step, n_hid), f32)
        g_att = jnp.zeros((step, n_att), f32)
        for k in range(n_f):
            c = c_ref[:, columns(at_ref, k, n_f, rows)]
            wd, wo = down_out(ins[2:], k)
            g_act = g_act + mm(c, wd)
            g_att = g_att + mm(c, wo)
        pre = (g_act * slope_ref[...].astype(f32)).astype(bf16)
        pre_ref[...] = pre
        do_ref[...] = g_att.astype(bf16)
        total = jnp.broadcast_to(jnp.sum(pre.astype(f32), axis=0, keepdims=True), (8, n_hid))

        @pl.when(pl.program_id(0) == 0)
        def _():
            sum_ref[...] = total

        @pl.when(pl.program_id(0) > 0)
        def _():
            sum_ref[...] += total

    def down_back(c, slope):
        return run(
            down_back_kernel,
            [array((length, n_hid), bf16), array((length, n_att), bf16), array((8, n_hid), f32)],
            tok_grid,
            [rows_of(step, width), rows_of(step, n_hid)] + do_specs,
            [rows_of(step, n_hid), rows_of(step, n_att), fixed(8, n_hid)],
            [c, slope, w_down, w_out, *got_do],
            name="down_back",
        )

    def back_kernel(at_ref, ins, outs, scratch):
        dqkv_ref, dpre_ref, vec_ref = ins[:3]
        wq, wk, wv = ins[3:6]
        w_other, wu = ins[6 : 5 + n_f], ins[5 + n_f :]
        for k in range(n_f):
            cols = columns(at_ref, k, n_f, rows)
            if k == 0:
                first = mm_rows(dqkv_ref[:, :n_att], wq[...])
                first = first + mm_rows(dqkv_ref[:, n_att : 2 * n_att], wk[...])
                first = first + mm_rows(dqkv_ref[:, 2 * n_att :], wv[...])
            else:
                first = mm_rows(dqkv_ref[...], w_other[k - 1][...])
            second = mm_rows(dpre_ref[...], wu[k][...])
            outs[0][:, cols] = (first * vec_ref[0:1, cols] + second * vec_ref[2:3, cols]).astype(bf16)

    def back(dqkv, dpre):
        return run(
            back_kernel,
            [array((length, width), bf16)],
            tok_grid,
            [rows_of(step, n_qkv), rows_of(step, n_hid), fixed(8, width)] + qkv_specs + u_specs,
            [rows_of(step, width)],
            [dqkv, dpre, vecs, *own_qkv, *got_qkv, w_up, *got_u],
            name="back",
        )[0]

    g_step = min(256, rows)
    per = rows // g_step

    def grads_kernel(n_pairs, n_w, chunks, at_ref, ins, outs, scratch):
        pieces = []
        for i in range(n_pairs):
            a0, a1, g0, g1 = ins[4 * i : 4 * i + 4]
            pieces.append(mm_tokens(a0[...], g0[...]) + mm_tokens(a1[...], g1[...]))
        start = 0
        full = pieces[0] if n_pairs == 1 else jnp.concatenate(pieces, axis=1)
        for out, n in zip(outs, chunks):
            out[...] = full[:, start : start + n].astype(out.dtype)
            start += n
        if n_w:
            weights = ins[4 * n_pairs : 4 * n_pairs + n_w]
            sums = ins[4 * n_pairs + n_w :]
            g_sum = sums[0][0:1] + sums[1][0:1]
            gain = jnp.zeros((g_step, 1), f32)
            shift = jnp.zeros((g_step, 1), f32)
            start = 0
            for w_ref in weights:
                w = w_ref[...].astype(f32)
                n = w.shape[1]
                gain = gain + jnp.sum(w * full[:, start : start + n], axis=1, keepdims=True)
                shift = shift + jnp.sum(w * g_sum[:, start : start + n], axis=1, keepdims=True)
                start += n
            lane = lax.broadcasted_iota(jnp.int32, (g_step, LANES), 1)
            outs[-1][...] = jnp.where(lane == 0, gain, jnp.where(lane == 1, shift, 0.0))

    def grads(pairs, chunks, k, weights, sums, name):
        def left(i, at):
            return (0, rem(at[F_AT] + k, n_f) * per + i)

        specs, operands = [], []
        for (a0, a1), (g0, g1) in pairs:
            specs += [pl.BlockSpec((length, g_step), left)] * 2 + [fixed(length, g0.shape[1])] * 2
            operands += [a0, a1, g0, g1]
        if weights:
            for w, n in weights:
                if k == 0:
                    specs.append(pl.BlockSpec((g_step, n), lambda i, at: (i, at[J_AT])))
                else:
                    specs.append(pl.BlockSpec((g_step, n), lambda i, at: (i, 0)))
                operands.append(w)
            specs += [fixed(8, s.shape[1]) for s in sums]
            operands += list(sums)
        outs = [array((rows, n), f32 if k == 0 else bf16) for n in chunks]
        out_specs = [rows_of(g_step, n) for n in chunks]
        if weights:
            outs.append(array((rows, LANES), f32))
            out_specs.append(rows_of(g_step, LANES))
        return run(
            functools.partial(grads_kernel, len(pairs), len(weights), chunks),
            outs,
            (per,),
            specs,
            out_specs,
            operands,
            name=name,
        )

    y_rows = rows // n_y
    y_step = min(256, y_rows)
    y_per = y_rows // y_step

    def grads_y_kernel(at_ref, ins, outs, scratch):
        a0, a1, g0, g1 = ins[:4]
        weights, sums = ins[4 : 4 + n_f], ins[4 + n_f :]
        full = mm_tokens(a0[...], g0[...]) + mm_tokens(a1[...], g1[...])
        outs[0][...] = full.astype(outs[0].dtype)
        part_at = pl.program_id(0) // y_per
        w = weights[0][...].astype(f32)
        for q in range(1, n_f):
            w = jnp.where(part_at == q, weights[q][...].astype(f32), w)
        gain = jnp.sum(w * full, axis=1, keepdims=True)
        shift = jnp.sum(w * (sums[0][0:1] + sums[1][0:1]), axis=1, keepdims=True)
        lane = lax.broadcasted_iota(jnp.int32, (y_step, LANES), 1)
        outs[1][...] = jnp.where(lane == 0, gain, jnp.where(lane == 1, shift, 0.0))

    def grads_y(left, right, k, own_w, other_w, sums, name):
        n = right[0].shape[1]

        def offset(i, at):
            return rem(at[Y_AT] + k, n_y) * y_per + rem(i, y_per)

        def columns_at(i, at):
            return (0, rem(at[F_AT] + i // y_per, n_f) * (rows // y_step) + offset(i, at))

        weights = [own_w] + [other_w[n_f - q - 1] for q in range(1, n_f)]
        specs = [pl.BlockSpec((length, y_step), columns_at)] * 2 + [fixed(length, n)] * 2
        specs.append(pl.BlockSpec((y_step, n), lambda i, at: (offset(i, at), at[J_AT])))
        specs += [pl.BlockSpec((y_step, n), lambda i, at: (offset(i, at), 0))] * (n_f - 1)
        specs += [fixed(8, n)] * 2
        return run(
            grads_y_kernel,
            [array((n_f * y_rows, n), f32 if k == 0 else bf16), array((n_f * y_rows, LANES), f32)],
            (n_f * y_per,),
            specs,
            [rows_of(y_step, n), rows_of(y_step, LANES)],
            [*left, *right, *weights, *sums],
            name=name,
        )

    bufs = {}
    out_width = {"q": width, "k": width, "v": width, "o": width, "u": hidden, "d": hidden}

    def place_kernel(widths, at_ref, ins, outs, scratch):
        start = 0
        for out, w in zip(outs, widths):
            out[...] = ins[0][0, :, start : start + w].astype(f32)
            start += w

    def place(piece, y_from, crossed, targets):
        def out_spec(w, sub, subs):
            def index(i, at):
                core = (1 - at[C_AT]) if crossed else at[C_AT]
                return (rem(at[Y_AT] + n_y - y_from, n_y), (i * CORES + core) * subs + sub)

            return pl.BlockSpec((y_rows, w), index)

        names = [t[0] for t in targets]
        total = piece.shape[2]
        operands = [piece]
        aliases = {}
        for i, name in enumerate(names):
            if name in bufs:
                aliases[1 + len(operands)] = i
                operands.append(bufs[name])
        made = run(
            functools.partial(place_kernel, [t[1] for t in targets]),
            [array((rows, out_width[name]), f32) for name in names],
            (n_ctx,),
            [pl.BlockSpec((1, y_rows, total), lambda i, at: (i, 0, 0))] + [ANY] * (len(operands) - 1),
            [out_spec(*t[1:]) for t in targets],
            operands,
            aliases=aliases,
            name="place",
            limit=16,
        )
        for name, m in zip(names, made):
            bufs[name] = m

    def rsy(terms):
        return add(terms, bf16, "sum_pairs")

    def halves_kernel(at_ref, ins, outs, scratch):
        total = ins[0][...].astype(f32)
        for r in ins[1:]:
            total = total + r[...].astype(f32)
        for h in range(2):

            @pl.when(pl.program_id(0) == h)
            def _(h=h):
                outs[h][...] = total.astype(bf16)

    def rsy_halves(terms):
        n, w = terms[0].shape
        return run(
            halves_kernel,
            [array((n, w // 2), bf16)] * 2,
            (2,),
            [pl.BlockSpec((n, w // 2), lambda i, at: (0, i))] * len(terms),
            [fixed(n, w // 2)] * 2,
            terms,
            name="sum_pairs",
            limit=16,
        )

    def gather_z(piece):
        return lax.all_gather(piece, "ctx", axis=0, tiled=False)

    d_halves = [[("d", half_hid, h, 2)] for h in range(2)]
    qk_at = [("q", n_att, 0, 1), ("k", n_att, 0, 1)]
    vo_at = [("v", n_att, 0, 1), ("o", n_att, 0, 1)]

    first_in, second_in, act, slope, qkv = zip(forward(tok[0]), forward(tok[1]))
    att, lse = zip(attend(qkv[0]), attend(qkv[1]))
    mixed_other = core_swap(branch(act[1], att[1]))
    mixed_own = branch(act[0], att[0])
    mixed_terms = [to_owners(mixed_own, mixed_other, "sum_mixed")]
    pre0, do0, up_sum0 = down_back(cot[0], slope[0])
    down_sent = [grads([(cot, act)], [half_hid] * 2, k, [], [], "grad_down") for k in range(1, n_f)]
    down_got = [[over_f(p[0], k + 1) for k, p in enumerate(down_sent)]]
    down_own = grads([(cot, act)], [half_hid] * 2, 0, [], [], "grad_down")
    down_got.append([over_f(pin(p[1]), k + 1) for k, p in enumerate(down_sent)])
    pre1, do1, up_sum1 = down_back(cot[1], slope[1])
    pre, up_sums = (pre0, pre1), (up_sum0, up_sum1)

    def grads_up(k):
        return grads_y(second_in, pre, k, w_up, got_u, up_sums, "grad_up")

    def grads_att(k):
        return grads(
            [(first_in, dqkv), (cot, att)],
            [4 * n_att],
            k,
            [(w, n_att) for w in own_qkv] if k == 0 else [(got_qkv[n_f - k - 1], n_qkv)],
            qkv_sums,
            "grad_att",
        )

    def sent(parts):
        chunks = len(parts[0]) - 1
        return [[over_f(p[i], k + 1) for k, p in enumerate(parts)] for i in range(chunks)], [p[-1] for p in parts]

    def rsx(own, got):
        made = split_sum([own] + got, n_y, Y_AT, "sum_fsdp")
        return [made[0]] + [over_y(made[k], k) for k in range(1, n_y)]

    y_terms = [None] * 6
    z = [None] * 5
    targets = [d_halves[0], d_halves[1], [("u", n_hid, 0, 1)], qk_at, vo_at]
    def after_z(i, over=True):
        piece = pin(z[i])
        return piece, core_swap(piece), ([over_y(piece, k) for k in range(1, n_y)] if over else [])

    def after_y(pieces, after=()):
        pieces = [pin(p, after) for p in pieces]
        return [(p, core_swap(p)) for p in pieces]

    def place_own(i, piece, crossed, y_from=0):
        place(piece, y_from, False, targets[i])
        place(crossed, y_from, True, targets[i])

    def place_over(i, pieces):
        for k, (piece, crossed) in enumerate(pieces):
            place_own(i, piece, crossed, k + 1)

    o_step = min(64, block_rows)
    o_grid = (block_rows // o_step,)

    def mixed_kernel(at_ref, ins, outs, scratch):
        total = ins[0][...].astype(f32) + ins[1][0:1]
        for r in ins[2:]:
            total = total + r[...].astype(f32)
        outs[0][...] = total.astype(bf16)

    def make_mixed(mixed_terms):
        return run(
        mixed_kernel,
        [array((block_rows, width), bf16)],
        o_grid,
        [rows_of(o_step, width), fixed(8, width)] + [rows_of(o_step, width)] * len(mixed_terms),
        [rows_of(o_step, width)],
        [tokens[0], bias_last, *mixed_terms],
        name="mixed",
    )[0]

    def tokens_kernel(at_ref, ins, outs, scratch):
        g = ins[2][...].astype(f32)
        for r in ins[3:]:
            g = g + r[...].astype(f32)
        x = ins[0][...].astype(f32)
        center = x - jnp.mean(x, axis=-1, keepdims=True)
        inv = lax.rsqrt(jnp.mean(center * center, axis=-1, keepdims=True) + norm_eps)
        n = center * inv
        inner = g - jnp.mean(g, axis=-1, keepdims=True) - n * jnp.mean(g * n, axis=-1, keepdims=True)
        outs[0][...] = ins[1][...].astype(f32) + inv * inner

    def make_grad_tokens(back_terms):
        return run(
        tokens_kernel,
        [array((block_rows, width), f32)],
        o_grid,
        [rows_of(o_step, width)] * (2 + len(back_terms)),
        [rows_of(o_step, width)],
        [tokens[0], cotangent[0], *back_terms],
        name="grad_tokens",
    )[0]
    y_d0 = rsx(down_own[0], down_got[0])
    up_sent = [grads_up(k) for k in range(1, n_y)]
    up_got = [over_y(p[0], k + 1) for k, p in enumerate(up_sent)]
    z[0] = gather_z(rsy(y_d0))
    dqkv0, qkv_sum0 = attend_back(qkv[0], do0, lse[0])
    dqkv1, qkv_sum1 = attend_back(qkv[1], do1, lse[1])
    dqkv, qkv_sums = (dqkv0, dqkv1), (qkv_sum0, qkv_sum1)
    up_own = grads_up(0)
    dots_u = [up_own[1]] + [p[1] for p in up_sent]
    y_d1 = rsx(down_own[1], down_got[1])
    mixed = make_mixed(mixed_terms)
    att_own = grads_att(0)
    up_split = split_sum([up_own[0]] + up_got, n_f, None, "sum_fsdp")
    x_u = [up_split[0]] + [over_f(up_split[k], k) for k in range(1, n_f)]
    z[1] = gather_z(rsy(y_d1))
    p0, c0, o0 = after_z(0)
    att_got, att_dots = sent([grads_att(k) for k in range(1, n_f)])
    dots_a = [att_own[-1]] + att_dots
    def norm_grads(dots, gain, shift):
        ordered = dots[0] if n_f == 1 else None
        if n_f == 2:
            pair = jnp.stack([d[:, :2] for d in dots])
            ordered = jnp.stack([jnp.where(f_idx == m, pair[0], pair[1]) for m in range(2)])
        elif n_f > 2:
            ordered = jnp.roll(jnp.stack([d[:, :2] for d in dots]), f_idx, axis=0)
        ordered = ordered.reshape(width, -1)
        return (ordered[:, 0] - shift * ordered[:, 1]) / gain, ordered[:, 1]

    g_gain1, g_shift1 = norm_grads(dots_a, gain1, shift1)
    def by_rows(dots):
        cut = [d[:, :2].reshape(n_f, y_rows, 2) for d in dots]
        parts = [
            functools.reduce(lambda so_far, k: jnp.where(jnp.mod(m - y_idx, n_y) == k, cut[k], so_far), range(1, n_y), cut[0])
            for m in range(n_y)
        ]
        return list(jnp.stack(parts, axis=1).reshape(n_f, rows, 2))

    g_gain2, g_shift2 = norm_grads(by_rows(dots_u), gain2, shift2)
    qkv_sum = qkv_sum0[0] + qkv_sum1[0]
    up_sum = up_sum0[0] + up_sum1[0]

    def spot(vec, size):
        return lax.dynamic_update_slice_in_dim(jnp.zeros((size,), f32), vec, j_idx * vec.shape[0], axis=0)

    sums = [
        g_gain1,
        g_shift1,
        g_gain2,
        g_shift2,
        spot(qkv_sum[:n_att], width),
        spot(qkv_sum[n_att : n_att + ROT], heads * ROT),
        spot(qkv_sum[2 * n_att :], width),
        jnp.sum(cotangent[0].astype(f32), axis=0),
        spot(up_sum, hidden),
    ]
    vec = jnp.concatenate(sums).reshape(-1, LANES)

    vec = pin(vec)
    place_own(0, p0, c0)
    back_other = core_swap(back(dqkv[1], pre[1]))
    p1, c1, o1 = after_z(1)
    o0 = after_y(o0)
    z[2] = gather_z(rsy(x_u))
    place_own(1, p1, c1)
    place_over(0, o0)
    back_own = back(dqkv[0], pre[0])
    vec_f = [vec] + [over_f(vec, k) for k in range(1, n_f)]
    y_a = rsx(att_own[0], att_got[0])
    o1 = after_y(o1)
    vec = add(vec_f, f32, "sum_small")
    vec_c = [vec, core_swap(vec)]
    vec = add(vec_c, f32, "sum_small")
    vec_y = [vec] + [over_y(vec, k) for k in range(1, n_y)]
    vec = add(vec_y, f32, "sum_small")
    z[3], z[4] = [gather_z(p) for p in rsy_halves(y_a)]
    p2, c2, o2 = after_z(2)
    place_own(2, p2, c2)
    place_over(1, o1)
    back_terms = [to_owners(back_own, back_other, "sum_back")]
    o2 = after_y(o2)
    p3, c3, o3 = after_z(3)
    vec_z = [vec, lax.ppermute(vec, "ctx", [(0, 1), (1, 0), (2, 3), (3, 2)])]
    place_own(3, p3, c3)
    place_over(2, o2)
    vec = add(vec_z, f32, "sum_small")
    vec_z = [vec, lax.ppermute(vec, "ctx", [(0, 2), (2, 0), (1, 3), (3, 1)])]
    p4, c4, o4 = after_z(4)
    o3 = after_y(o3)
    place_own(4, p4, c4)
    place_over(3, o3)
    vec = add(vec_z, f32, "sum_small").reshape(-1)
    outs = []
    start = 0
    for s in sums:
        size = s.shape[0] // n_f
        outs.append(lax.dynamic_slice_in_dim(vec, start + f_idx * size, size, axis=0))
        start += s.shape[0]
    s_g1, s_b1, s_g2, s_b2, s_q, s_k, s_v, s_last, s_u = outs

    grad_tokens = make_grad_tokens(back_terms)
    o4 = after_y(o4, outs)
    place_over(4, o4)

    return (
        mixed[None],
        grad_tokens[None],
        s_g1,
        s_b1,
        s_g2,
        s_b2,
        bufs["q"],
        bufs["k"],
        bufs["v"],
        s_q,
        s_k,
        s_v,
        bufs["o"],
        s_last,
        bufs["u"],
        s_u,
        bufs["d"],
        s_last,
    )


def solution(mesh):
    seq = P(("dp", "fsdp"), "ctx", None)
    vec, mat = P("fsdp"), P("fsdp", None)
    params_in = (vec,) * 4 + (mat,) * 3 + (vec,) * 3 + (mat, vec, mat, vec, mat, vec)
    return jax.shard_map(
        functools.partial(local, mesh.shape["dp"], mesh.shape["ctx"], mesh.shape["fsdp"]),
        mesh=mesh,
        in_specs=(seq, seq) + params_in,
        out_specs=(seq, seq) + params_in,
        check_vma=False,
    )
```

```python
import functools
import math

import jax
import jax.numpy as jnp
from jax import lax
from jax.experimental import pallas as pl
from jax.experimental.pallas import tpu as pltpu
from jax.sharding import PartitionSpec as P

HEAD_DIM = 256
ROT = 64
HALF = ROT // 2
LANES = 128
CORES = 2
norm_eps = 1e-05
masked_score = -1e30
MIB = 1 << 20
f32 = jnp.float32
bf16 = jnp.bfloat16
SCALE = 1.0 / math.sqrt(HEAD_DIM)
F_AT, J_AT, Y_AT, Z_AT, C_AT = range(5)


def dot(left, right, dims):
    return lax.dot_general(left, right, (dims, ((), ())), preferred_element_type=f32)


def mm(left, right):
    return dot(left, right, ((1,), (0,)))


def mm_rows(left, right):
    return dot(left, right, ((1,), (1,)))


def mm_tokens(left, right):
    return dot(left, right, ((0,), (0,)))


def array(shape, dtype):
    return jax.ShapeDtypeStruct(shape, dtype)


ANY = pl.BlockSpec(memory_space=pl.ANY)
PLANNED = {
    "join": 2,
    "forward": 18,
    "attend": 2,
    "branch": 10,
    "sum_mixed": 4,
    "down_back": 10,
    "grad_down": 9,
    "grad_up": 9,
    "grad_att": 9,
    "attend_back": 6,
    "back": 13,
    "sum_back": 4,
    "sum_fsdp": 2,
    "sum_pairs": 8,
    "sum_small": 1,
    "pin": 15,
    "place": 4,
    "mixed": 3,
    "grad_tokens": 4,
    "stack": 2,
}


class Chain:
    def __init__(self, at):
        self.at = at
        self.last = None

    def __call__(self, kernel, outs, grid, in_specs, out_specs, operands, aliases=None, scratch=(), name=None, limit=50, after=()):
        n_in, n_out = len(operands), len(outs)
        extra = ([] if self.last is None else [self.last]) + list(after)

        def body(at_ref, *refs):
            ins = refs[:n_in]
            made = refs[n_in + len(extra) :]
            kernel(at_ref, ins, made[:n_out], made[n_out + 1 :])

        result = pl.pallas_call(
            body,
            out_shape=tuple(outs) + (array((8, LANES), f32),),
            grid_spec=pltpu.PrefetchScalarGridSpec(
                num_scalar_prefetch=1,
                grid=grid,
                in_specs=list(in_specs) + [ANY] * len(extra),
                out_specs=list(out_specs) + [ANY],
                scratch_shapes=list(scratch),
            ),
            input_output_aliases=aliases or {},
            compiler_params=pltpu.CompilerParams(vmem_limit_bytes=limit * MIB),
            cost_estimate=pl.CostEstimate(
                flops=int(1.15e4 * PLANNED[name]), bytes_accessed=1, transcendentals=0
            ),
            name=name,
        )(self.at, *operands, *extra)
        self.last = result[-1]
        return result[:-1]


def rem(a, n):
    return lax.rem(a, jnp.int32(n))


def columns(at_ref, k, n_f, rows):
    block = rem(at_ref[F_AT] + n_f - k, n_f)
    return pl.ds(pl.multiple_of(block * rows, rows), rows)


def turn(v, cos_t, sin_a, sin_b):
    low = v[:, :LANES]
    low = low * cos_t + pltpu.roll(low, LANES - HALF, 1) * sin_a + pltpu.roll(low, HALF, 1) * sin_b
    return jnp.concatenate([low, v[:, LANES:]], axis=1)


def shift_perm(count, step):
    return [(i, (i + step) % count) for i in range(count)]


def local(
    n_dp,
    n_ctx,
    n_f,
    tokens,
    cotangent,
    norm1_gain,
    norm1_bias,
    norm2_gain,
    norm2_bias,
    w_query,
    w_key,
    w_value,
    b_query,
    b_key,
    b_value,
    w_out,
    b_out,
    w_up,
    b_up,
    w_down,
    b_down,
):
    n_y = n_dp // CORES
    dp_idx, z_idx, f_idx = lax.axis_index("dp"), lax.axis_index("ctx"), lax.axis_index("fsdp")
    y_idx, c_idx = dp_idx // CORES, dp_idx % CORES
    splits = n_ctx * CORES
    j_idx = z_idx * CORES + c_idx
    block_rows, width = tokens.shape[1], tokens.shape[2]
    length = block_rows * n_ctx
    hidden = w_up.shape[1]
    heads = width // HEAD_DIM
    rows = width // n_f
    n_att, n_hid = width // splits, hidden // splits
    assert n_att == HEAD_DIM and n_ctx == 4
    n_qkv = 3 * n_att
    half_hid = n_hid // 2
    at = jnp.stack([f_idx, j_idx, y_idx, z_idx, c_idx]).astype(jnp.int32)
    run = Chain(at)

    def core_swap(value):
        return lax.ppermute(value, "dp", [(i, i ^ 1) for i in range(n_dp)])

    def over_y(value, step):
        return lax.ppermute(value, "dp", shift_perm(n_dp, CORES * step))

    def over_z(value, step):
        return lax.ppermute(value, "ctx", shift_perm(n_ctx, step))

    def over_f(value, step):
        return lax.ppermute(value, "fsdp", shift_perm(n_f, step))

    def mine(w, n):
        return lax.dynamic_slice_in_dim(w, j_idx * n, n, axis=1)

    small = [norm1_gain, norm1_bias, norm2_gain, norm2_bias, b_query, b_key, b_value, b_out + b_down, b_up]
    sizes = [s.shape[0] for s in small]
    ends = [sum(sizes[:i]) for i in range(len(sizes) + 1)]
    small_own = jnp.concatenate(small)
    small_got = [small_own] + [over_f(small_own, k) for k in range(1, n_f)]

    own_tok = lax.all_gather(tokens[0], "ctx", axis=0, tiled=True)
    own_cot = lax.all_gather(cotangent[0], "ctx", axis=0, tiled=True)
    cot = (own_cot, core_swap(own_cot))

    def pin(value, after=()):
        return run(lambda *a: None, [array(value.shape, value.dtype)], (1,), [ANY], [ANY], [value], aliases={1: 0}, name="pin", limit=4, after=after)[0]

    def fetch(part):
        return [over_f(part, k) for k in range(1, n_f)]

    y_part = rows // n_y
    got_u = fetch(lax.dynamic_slice(w_up, (y_idx * y_part, j_idx * n_hid), (y_part, n_hid)))
    got_qkv = fetch(jnp.concatenate([mine(w_query, n_att), mine(w_key, n_att), mine(w_value, n_att)], axis=1))
    got_do = fetch(jnp.concatenate([mine(w_down, n_hid), mine(w_out, n_att)], axis=1))

    def whole(i):
        pieces = [g[ends[i] : ends[i + 1]] for g in small_got]
        if n_f == 2:
            return jnp.concatenate([jnp.where(f_idx == m, pieces[0], pieces[1]) for m in range(2)])
        rolled = jnp.stack(pieces[::-1])
        return jnp.roll(rolled, f_idx + 1, axis=0).reshape(-1)

    gain1, shift1, gain2, shift2, bq, bk, bv, b_last, bu = [whole(i) for i in range(len(small))]

    def part(vec, n):
        return lax.dynamic_slice_in_dim(vec, j_idx * n, n, axis=0)

    def eight(vec):
        return jnp.broadcast_to(vec[None], (8, vec.shape[0]))

    vecs = jnp.concatenate([jnp.stack([gain1, shift1, gain2, shift2]), jnp.zeros((4, width), f32)])
    key_shift = jnp.pad(part(bk, ROT), (0, HEAD_DIM - ROT))
    bias_qkv = eight(jnp.concatenate([part(bq, n_att), key_shift, part(bv, n_att)]))
    bias_up = eight(part(bu, n_hid))
    bias_last = eight(b_last)
    positions = jnp.arange(length, dtype=f32)
    inverse = 10000.0 ** (-2.0 * jnp.arange(HALF, dtype=f32) / ROT)
    angles = positions[:, None] * inverse[None, :]
    cosine, sine = jnp.cos(angles), jnp.sin(angles)
    none = jnp.zeros((length, LANES - ROT), f32)
    zero = jnp.zeros_like(sine)
    tables = (
        jnp.concatenate([cosine, cosine, none + 1.0], axis=1),
        jnp.concatenate([-sine, zero, none], axis=1),
        jnp.concatenate([zero, sine, none], axis=1),
    )

    def join_kernel(at_ref, ins, outs, scratch):
        for k, r in enumerate(ins):

            @pl.when(pl.program_id(0) == k)
            def _(r=r):
                outs[0][0] = r[...]

    def share(piece):
        piece = pin(piece)
        parts = [piece] + [over_y(piece, k) for k in range(1, n_y)]
        joined = run(
            join_kernel,
            [array((n_y, y_part, n_hid), bf16)],
            (n_y,),
            [pl.BlockSpec((y_part, n_hid), lambda i, at: (0, 0))] * n_y,
            [pl.BlockSpec((1, y_part, n_hid), lambda i, at: (rem(at[Y_AT] + n_y - i, n_y), 0, 0))],
            parts,
            name="join",
            limit=16,
        )[0]
        return joined.reshape(rows, n_hid)

    vecs, bias_qkv, bias_up = pin(vecs), pin(bias_qkv), pin(bias_up)
    tables = tuple(pin(t) for t in tables)
    got_u = [share(g) for g in got_u]
    own_tok = pin(own_tok)
    tok = ([own_tok], [core_swap(own_tok[m * block_rows : (m + 1) * block_rows]) for m in range(n_ctx)])

    def rows_of(n, w):
        return pl.BlockSpec((n, w), lambda i, at: (i, 0))

    def fixed(n, w):
        return pl.BlockSpec((n, w), lambda i, at: (0, 0))

    def column(n, w):
        return pl.BlockSpec((n, w), lambda i, at: (0, at[J_AT]))

    own_qkv = [w_query, w_key, w_value]
    qkv_specs = [column(rows, n_att)] * 3 + [fixed(rows, n_qkv)] * (n_f - 1)
    u_specs = [column(rows, n_hid)] + [fixed(rows, n_hid)] * (n_f - 1)
    do_specs = [column(rows, n_hid), column(rows, n_att)] + [fixed(rows, n_hid + n_att)] * (n_f - 1)
    step = min(256, length)
    tok_grid = (length // step,)
    n_vec = len(tables)

    def forward_kernel(n_x, at_ref, ins, outs, scratch):
        x_refs, ins = ins[:n_x], ins[n_x:]
        vec_ref, cos_ref, sa_ref, sb_ref, bqkv_ref, bu_ref = ins[:6]
        wu = ins[6 : 6 + n_f]
        wq, wk, wv = ins[6 + n_f : 9 + n_f]
        w_other = ins[9 + n_f :]
        a1_ref, a2_ref, act_ref, slope_ref, qkv_ref = outs

        def normalize(x_ref):
            x = x_ref[...].astype(f32)
            center = x - jnp.mean(x, axis=-1, keepdims=True)
            spread = jnp.mean(center * center, axis=-1, keepdims=True)
            n = center * lax.rsqrt(spread + norm_eps)
            a1_ref[...] = (n * vec_ref[0:1] + vec_ref[1:2]).astype(bf16)
            a2_ref[...] = (n * vec_ref[2:3] + vec_ref[3:4]).astype(bf16)

        each = length // step // n_x
        for m, x_ref in enumerate(x_refs):
            if n_x == 1:
                normalize(x_ref)
            else:
                pl.when(pl.program_id(0) // each == m)(functools.partial(normalize, x_ref))
        h = jnp.broadcast_to(bu_ref[0:1], (step, n_hid))
        for k in range(n_f):
            h = h + mm(a2_ref[:, columns(at_ref, k, n_f, rows)], wu[k][...])
        cdf = 0.5 * (1.0 + lax.erf(h * (1.0 / math.sqrt(2.0))))
        pdf = jnp.exp(-0.5 * h * h) * (1.0 / math.sqrt(2.0 * math.pi))
        act_ref[...] = (h * cdf).astype(bf16)
        slope_ref[...] = (cdf + h * pdf).astype(bf16)
        cos_t, sa, sb = cos_ref[...], sa_ref[...], sb_ref[...]
        for m, w_own in enumerate((wq, wk, wv)):
            lanes = slice(m * n_att, (m + 1) * n_att)
            v = mm(a1_ref[:, columns(at_ref, 0, n_f, rows)], w_own[...]) + bqkv_ref[0:1, lanes]
            for k in range(1, n_f):
                v = v + mm(a1_ref[:, columns(at_ref, k, n_f, rows)], w_other[k - 1][:, lanes])
            qkv_ref[:, lanes] = (turn(v, cos_t, sa, sb) if m < 2 else v).astype(bf16)

    def forward(xs):
        each = length // step // len(xs)

        def rows_in(m):
            return pl.BlockSpec((step, width), lambda i, at: (jnp.clip(i - m * each, 0, each - 1), 0))

        return run(
            functools.partial(forward_kernel, len(xs)),
            [array((length, width), bf16)] * 2 + [array((length, n_hid), bf16)] * 2 + [array((length, n_qkv), bf16)],
            tok_grid,
            [rows_in(m) for m in range(len(xs))]
            + [fixed(8, width)]
            + [rows_of(step, LANES)] * n_vec
            + [fixed(8, n_qkv), fixed(8, n_hid)]
            + u_specs
            + qkv_specs,
            [rows_of(step, width)] * 2 + [rows_of(step, n_hid)] * 2 + [rows_of(step, n_qkv)],
            [*xs, vecs, *tables, bias_qkv, bias_up, w_up, *got_u, *own_qkv, *got_qkv],
            name="forward",
        )

    q_block = min(256, length)

    def masked(lo, hi):
        rows_at = lo + lax.broadcasted_iota(jnp.int32, (hi - lo, hi), 0)
        return lax.broadcasted_iota(jnp.int32, (hi - lo, hi), 1) <= rows_at

    def attend_kernel(at_ref, ins, outs, scratch):
        (qkv_ref,) = ins
        att_ref, lse_ref = outs
        for lo in range(0, length, q_block):
            hi = lo + q_block
            s = mm_rows(qkv_ref[lo:hi, :n_att], qkv_ref[:hi, n_att : 2 * n_att]) * SCALE
            allowed = masked(lo, hi)
            s = jnp.where(allowed, s, masked_score)
            top = jnp.max(s, axis=-1, keepdims=True)
            e = jnp.where(allowed, jnp.exp(s - top), 0.0)
            total = jnp.sum(e, axis=-1, keepdims=True)
            att_ref[lo:hi] = (mm(e.astype(bf16), qkv_ref[:hi, 2 * n_att :]) / total).astype(bf16)
            lse_ref[lo:hi] = jnp.broadcast_to(top + jnp.log(total), (q_block, LANES))

    def attend(qkv):
        return run(
            attend_kernel,
            [array((length, n_att), bf16), array((length, LANES), f32)],
            (1,),
            [fixed(length, n_qkv)],
            [fixed(length, n_att), fixed(length, LANES)],
            [qkv],
            name="attend",
        )

    def attend_back_kernel(at_ref, ins, outs, scratch):
        qkv_ref, do_ref, lse_ref, cos_ref, sa_ref, sb_ref = ins
        grad_ref, sum_ref = outs
        dk_acc, dv_acc = scratch
        q_sum = jnp.zeros((1, n_att), f32)
        for lo in range(0, length, q_block):
            hi = lo + q_block
            qi, ki, vi = qkv_ref[lo:hi, :n_att], qkv_ref[:hi, n_att : 2 * n_att], qkv_ref[:hi, 2 * n_att :]
            do = do_ref[lo:hi]
            s = mm_rows(qi, ki) * SCALE
            chance = jnp.where(masked(lo, hi), jnp.exp(s - lse_ref[lo:hi, 0:1]), 0.0)
            d_chance = mm_rows(do, vi)
            row_dot = jnp.sum(chance * d_chance, axis=-1, keepdims=True)
            ds = (chance * (d_chance - row_dot)).astype(bf16)
            dq = turn(mm(ds, ki) * SCALE, cos_ref[lo:hi], -sa_ref[lo:hi], -sb_ref[lo:hi]).astype(bf16)
            grad_ref[lo:hi, :n_att] = dq
            q_sum = q_sum + jnp.sum(dq.astype(f32), axis=0, keepdims=True)
            dk, dv = mm_tokens(ds, qi), mm_tokens(chance.astype(bf16), do)
            if lo > 0:
                dk_acc[:lo] += dk[:lo]
                dv_acc[:lo] += dv[:lo]
            dk_acc[lo:hi] = dk[lo:]
            dv_acc[lo:hi] = dv[lo:]
        dk = turn(dk_acc[...] * SCALE, cos_ref[...], -sa_ref[...], -sb_ref[...]).astype(bf16)
        dv = dv_acc[...].astype(bf16)
        grad_ref[:, n_att : 2 * n_att] = dk
        grad_ref[:, 2 * n_att :] = dv
        sums = (q_sum, jnp.sum(dk.astype(f32), axis=0, keepdims=True), jnp.sum(dv.astype(f32), axis=0, keepdims=True))
        for m, total in enumerate(sums):
            sum_ref[:, m * n_att : (m + 1) * n_att] = jnp.broadcast_to(total, (8, n_att))

    def attend_back(qkv, do, lse):
        return run(
            attend_back_kernel,
            [array((length, n_qkv), bf16), array((8, n_qkv), f32)],
            (1,),
            [fixed(length, n_qkv), fixed(length, n_att)] + [fixed(length, LANES)] * (1 + n_vec),
            [fixed(length, n_qkv), fixed(8, n_qkv)],
            [qkv, do, lse, *tables],
            scratch=[pltpu.VMEM((length, n_att), f32)] * 2,
            name="attend_back",
        )

    def down_out(refs, k):
        if k == 0:
            return refs[0][...], refs[1][...]
        return refs[1 + k][:, :n_hid], refs[1 + k][:, n_hid:]

    def branch_kernel(at_ref, ins, outs, scratch):
        act_ref, att_ref = ins[:2]
        for k in range(n_f):
            wd, wo = down_out(ins[2:], k)
            value = mm_rows(act_ref[...], wd) + mm_rows(att_ref[...], wo)
            outs[0][:, columns(at_ref, k, n_f, rows)] = value.astype(bf16)

    def branch(act, att):
        return run(
            branch_kernel,
            [array((length, width), bf16)],
            tok_grid,
            [rows_of(step, n_hid), rows_of(step, n_att)] + do_specs,
            [rows_of(step, width)],
            [act, att, w_down, w_out, *got_do],
            name="branch",
        )[0]

    def split_kernel(count, at_ref, ins, outs, scratch):
        for k in range(count):

            @pl.when(pl.program_id(0) == k)
            def _(k=k):
                total = ins[0][...].astype(f32)
                for r in ins[1:]:
                    total = total + r[...].astype(f32)
                outs[k][...] = total.astype(outs[k].dtype)

    def split_sum(values, count, where, name):
        n, w = values[0].shape
        spec = pl.BlockSpec((n // count, w), lambda i, at: (i if where is None else rem(at[where] + i, count), 0))
        return run(
            functools.partial(split_kernel, count),
            [array((n // count, w), f32 if k == 0 else bf16) for k in range(count)],
            (count,),
            [spec] * len(values),
            [fixed(n // count, w)] * count,
            values,
            name=name,
            limit=16,
        )

    def add_kernel(at_ref, ins, outs, scratch):
        total = ins[0][...].astype(f32)
        for r in ins[1:]:
            total = total + r[...].astype(f32)
        outs[0][...] = total.astype(outs[0].dtype)

    def add(values, dtype, name):
        n, w = values[0].shape
        m = n // 2 if n % 32 == 0 else n
        return run(
            add_kernel,
            [array((n, w), dtype)],
            (n // m,),
            [rows_of(m, w)] * len(values),
            [rows_of(m, w)],
            values,
            name=name,
            limit=16,
        )[0]

    def to_owners(own, other_got, name):
        return lax.psum_scatter(add([own, other_got], bf16, name), "ctx", scatter_dimension=0, tiled=True)

    def down_back_kernel(at_ref, ins, outs, scratch):
        c_ref, slope_ref = ins[:2]
        pre_ref, do_ref, sum_ref = outs
        g_act = jnp.zeros((step, n_hid), f32)
        g_att = jnp.zeros((step, n_att), f32)
        for k in range(n_f):
            c = c_ref[:, columns(at_ref, k, n_f, rows)]
            wd, wo = down_out(ins[2:], k)
            g_act = g_act + mm(c, wd)
            g_att = g_att + mm(c, wo)
        pre = (g_act * slope_ref[...].astype(f32)).astype(bf16)
        pre_ref[...] = pre
        do_ref[...] = g_att.astype(bf16)
        total = jnp.broadcast_to(jnp.sum(pre.astype(f32), axis=0, keepdims=True), (8, n_hid))

        @pl.when(pl.program_id(0) == 0)
        def _():
            sum_ref[...] = total

        @pl.when(pl.program_id(0) > 0)
        def _():
            sum_ref[...] += total

    def down_back(c, slope):
        return run(
            down_back_kernel,
            [array((length, n_hid), bf16), array((length, n_att), bf16), array((8, n_hid), f32)],
            tok_grid,
            [rows_of(step, width), rows_of(step, n_hid)] + do_specs,
            [rows_of(step, n_hid), rows_of(step, n_att), fixed(8, n_hid)],
            [c, slope, w_down, w_out, *got_do],
            name="down_back",
        )

    def back_kernel(at_ref, ins, outs, scratch):
        dqkv_ref, dpre_ref, vec_ref = ins[:3]
        wq, wk, wv = ins[3:6]
        w_other, wu = ins[6 : 5 + n_f], ins[5 + n_f :]
        for k in range(n_f):
            cols = columns(at_ref, k, n_f, rows)
            if k == 0:
                first = mm_rows(dqkv_ref[:, :n_att], wq[...])
                first = first + mm_rows(dqkv_ref[:, n_att : 2 * n_att], wk[...])
                first = first + mm_rows(dqkv_ref[:, 2 * n_att :], wv[...])
            else:
                first = mm_rows(dqkv_ref[...], w_other[k - 1][...])
            second = mm_rows(dpre_ref[...], wu[k][...])
            outs[0][:, cols] = (first * vec_ref[0:1, cols] + second * vec_ref[2:3, cols]).astype(bf16)

    def back(dqkv, dpre):
        return run(
            back_kernel,
            [array((length, width), bf16)],
            tok_grid,
            [rows_of(step, n_qkv), rows_of(step, n_hid), fixed(8, width)] + qkv_specs + u_specs,
            [rows_of(step, width)],
            [dqkv, dpre, vecs, *own_qkv, *got_qkv, w_up, *got_u],
            name="back",
        )[0]

    g_step = min(256, rows)
    per = rows // g_step

    def grads_kernel(n_pairs, n_w, chunks, at_ref, ins, outs, scratch):
        pieces = []
        for i in range(n_pairs):
            a0, a1, g0, g1 = ins[4 * i : 4 * i + 4]
            pieces.append(mm_tokens(a0[...], g0[...]) + mm_tokens(a1[...], g1[...]))
        start = 0
        full = pieces[0] if n_pairs == 1 else jnp.concatenate(pieces, axis=1)
        for out, n in zip(outs, chunks):
            out[...] = full[:, start : start + n].astype(out.dtype)
            start += n
        if n_w:
            weights = ins[4 * n_pairs : 4 * n_pairs + n_w]
            sums = ins[4 * n_pairs + n_w :]
            g_sum = sums[0][0:1] + sums[1][0:1]
            gain = jnp.zeros((g_step, 1), f32)
            shift = jnp.zeros((g_step, 1), f32)
            start = 0
            for w_ref in weights:
                w = w_ref[...].astype(f32)
                n = w.shape[1]
                gain = gain + jnp.sum(w * full[:, start : start + n], axis=1, keepdims=True)
                shift = shift + jnp.sum(w * g_sum[:, start : start + n], axis=1, keepdims=True)
                start += n
            lane = lax.broadcasted_iota(jnp.int32, (g_step, LANES), 1)
            outs[-1][...] = jnp.where(lane == 0, gain, jnp.where(lane == 1, shift, 0.0))

    def grads(pairs, chunks, k, weights, sums, name):
        def left(i, at):
            return (0, rem(at[F_AT] + k, n_f) * per + i)

        specs, operands = [], []
        for (a0, a1), (g0, g1) in pairs:
            specs += [pl.BlockSpec((length, g_step), left)] * 2 + [fixed(length, g0.shape[1])] * 2
            operands += [a0, a1, g0, g1]
        if weights:
            for w, n in weights:
                if k == 0:
                    specs.append(pl.BlockSpec((g_step, n), lambda i, at: (i, at[J_AT])))
                else:
                    specs.append(pl.BlockSpec((g_step, n), lambda i, at: (i, 0)))
                operands.append(w)
            specs += [fixed(8, s.shape[1]) for s in sums]
            operands += list(sums)
        outs = [array((rows, n), f32 if k == 0 else bf16) for n in chunks]
        out_specs = [rows_of(g_step, n) for n in chunks]
        if weights:
            outs.append(array((rows, LANES), f32))
            out_specs.append(rows_of(g_step, LANES))
        return run(
            functools.partial(grads_kernel, len(pairs), len(weights), chunks),
            outs,
            (per,),
            specs,
            out_specs,
            operands,
            name=name,
        )

    y_rows = rows // n_y
    y_step = min(256, y_rows)
    y_per = y_rows // y_step

    def grads_y_kernel(at_ref, ins, outs, scratch):
        a0, a1, g0, g1 = ins[:4]
        weights, sums = ins[4 : 4 + n_f], ins[4 + n_f :]
        full = mm_tokens(a0[...], g0[...]) + mm_tokens(a1[...], g1[...])
        outs[0][...] = full.astype(outs[0].dtype)
        part_at = pl.program_id(0) // y_per
        w = weights[0][...].astype(f32)
        for q in range(1, n_f):
            w = jnp.where(part_at == q, weights[q][...].astype(f32), w)
        gain = jnp.sum(w * full, axis=1, keepdims=True)
        shift = jnp.sum(w * (sums[0][0:1] + sums[1][0:1]), axis=1, keepdims=True)
        lane = lax.broadcasted_iota(jnp.int32, (y_step, LANES), 1)
        outs[1][...] = jnp.where(lane == 0, gain, jnp.where(lane == 1, shift, 0.0))

    def grads_y(left, right, k, own_w, other_w, sums, name):
        n = right[0].shape[1]

        def offset(i, at):
            return rem(at[Y_AT] + k, n_y) * y_per + rem(i, y_per)

        def columns_at(i, at):
            return (0, rem(at[F_AT] + i // y_per, n_f) * (rows // y_step) + offset(i, at))

        weights = [own_w] + [other_w[n_f - q - 1] for q in range(1, n_f)]
        specs = [pl.BlockSpec((length, y_step), columns_at)] * 2 + [fixed(length, n)] * 2
        specs.append(pl.BlockSpec((y_step, n), lambda i, at: (offset(i, at), at[J_AT])))
        specs += [pl.BlockSpec((y_step, n), lambda i, at: (offset(i, at), 0))] * (n_f - 1)
        specs += [fixed(8, n)] * 2
        return run(
            grads_y_kernel,
            [array((n_f * y_rows, n), f32 if k == 0 else bf16), array((n_f * y_rows, LANES), f32)],
            (n_f * y_per,),
            specs,
            [rows_of(y_step, n), rows_of(y_step, LANES)],
            [*left, *right, *weights, *sums],
            name=name,
        )

    bufs = {}
    out_width = {"q": width, "k": width, "v": width, "o": width, "u": hidden, "d": hidden}

    def place_kernel(widths, at_ref, ins, outs, scratch):
        start = 0
        for out, w in zip(outs, widths):
            out[...] = ins[0][0, 0, :, start : start + w].astype(f32)
            start += w

    def place(piece, y_from, crossed, targets):
        if piece.ndim == 3:
            piece = piece[:, None]
        stacked = piece.shape[1]

        def out_spec(w, sub, subs):
            def index(i, j, at):
                core = (1 - at[C_AT]) if crossed else at[C_AT]
                return (rem(at[Y_AT] + 2 * n_y - y_from - j, n_y), (i * CORES + core) * subs + sub)

            return pl.BlockSpec((y_rows, w), index)

        names = [t[0] for t in targets]
        total = piece.shape[3]
        operands = [piece]
        aliases = {}
        for i, name in enumerate(names):
            if name in bufs:
                aliases[1 + len(operands)] = i
                operands.append(bufs[name])
        made = run(
            functools.partial(place_kernel, [t[1] for t in targets]),
            [array((rows, out_width[name]), f32) for name in names],
            (n_ctx, stacked),
            [pl.BlockSpec((1, 1, y_rows, total), lambda i, j, at: (i, j, 0, 0))] + [ANY] * (len(operands) - 1),
            [out_spec(*t[1:]) for t in targets],
            operands,
            aliases=aliases,
            name="place",
            limit=20,
        )
        for name, m in zip(names, made):
            bufs[name] = m

    def rsy(terms):
        return add(terms, bf16, "sum_pairs")

    def cut_kernel(first, at_ref, ins, outs, scratch):
        total = ins[0][...].astype(f32)
        for r in ins[1:]:
            total = total + r[...].astype(f32)

        @pl.when(pl.program_id(0) < first)
        def _():
            outs[0][...] = total.astype(bf16)

        @pl.when(pl.program_id(0) >= first)
        def _():
            outs[1][...] = total.astype(bf16)

    def rsy_cut(terms, w):
        n, all_w = terms[0].shape
        first = all_w // w - 1
        return run(
            functools.partial(cut_kernel, first),
            [array((n, first * w), bf16), array((n, w), bf16)],
            (first + 1,),
            [pl.BlockSpec((n, w), lambda i, at: (0, i))] * len(terms),
            [
                pl.BlockSpec((n, w), lambda i, at: (0, jnp.minimum(i, first - 1))),
                pl.BlockSpec((n, w), lambda i, at: (0, 0)),
            ],
            terms,
            name="sum_pairs",
            limit=16,
        )

    def stack_kernel(at_ref, ins, outs, scratch):
        for m, r in enumerate(ins):

            @pl.when(pl.program_id(0) == m)
            def _(r=r):
                outs[0][0] = r[...]

    def stack(pieces):
        n, w = pieces[0].shape
        return run(
            stack_kernel,
            [array((len(pieces), n, w), bf16)],
            (len(pieces),),
            [fixed(n, w)] * len(pieces),
            [pl.BlockSpec((1, n, w), lambda i, at: (i, 0, 0))],
            pieces,
            name="stack",
            limit=16,
        )[0]

    def gather_z(piece):
        return lax.all_gather(piece, "ctx", axis=0, tiled=False)

    d_halves = [[("d", half_hid, h, 2)] for h in range(2)]
    qkv_at = [(name, n_att, 0, 1) for name in ("q", "k", "v")]

    first_in, second_in, act, slope, qkv = zip(forward(tok[0]), forward(tok[1]))
    att, lse = zip(attend(qkv[0]), attend(qkv[1]))
    mixed_other = core_swap(branch(act[1], att[1]))
    mixed_own = branch(act[0], att[0])
    mixed_terms = [to_owners(mixed_own, mixed_other, "sum_mixed")]
    pre0, do0, up_sum0 = down_back(cot[0], slope[0])
    down_sent = [grads([(cot, act)], [half_hid] * 2, k, [], [], "grad_down") for k in range(1, n_f)]
    down_got = [[over_f(p[0], k + 1) for k, p in enumerate(down_sent)]]
    down_own = grads([(cot, act)], [half_hid] * 2, 0, [], [], "grad_down")
    down_got.append([over_f(pin(p[1]), k + 1) for k, p in enumerate(down_sent)])
    pre1, do1, up_sum1 = down_back(cot[1], slope[1])
    pre, up_sums = (pre0, pre1), (up_sum0, up_sum1)

    def grads_up(k):
        return grads_y(second_in, pre, k, w_up, got_u, up_sums, "grad_up")

    def grads_att(k):
        return grads(
            [(first_in, dqkv), (cot, att)],
            [4 * n_att],
            k,
            [(w, n_att) for w in own_qkv] if k == 0 else [(got_qkv[n_f - k - 1], n_qkv)],
            qkv_sums,
            "grad_att",
        )

    def sent(parts):
        chunks = len(parts[0]) - 1
        return [[over_f(p[i], k + 1) for k, p in enumerate(parts)] for i in range(chunks)], [p[-1] for p in parts]

    def rsx(own, got):
        made = split_sum([own] + got, n_y, Y_AT, "sum_fsdp")
        return [made[0]] + [over_y(made[k], k) for k in range(1, n_y)]

    y_terms = [None] * 6
    z = [None] * 5
    targets = [d_halves[0], d_halves[1], [("u", n_hid, 0, 1)], qkv_at, [("o", n_att, 0, 1)]]
    def after_z(i, over=True):
        piece = pin(z[i])
        return piece, core_swap(piece), ([over_y(piece, k) for k in range(1, n_y)] if over else [])

    def after_y(pieces, after=()):
        pieces = [pin(p, after) for p in pieces]
        return [(p, core_swap(p)) for p in pieces]

    def place_own(i, piece, crossed, y_from=0):
        place(piece, y_from, False, targets[i])
        place(crossed, y_from, True, targets[i])

    def place_over(i, pieces):
        for k, (piece, crossed) in enumerate(pieces):
            place_own(i, piece, crossed, k + 1)

    o_step = min(64, block_rows)
    o_grid = (block_rows // o_step,)

    def mixed_kernel(at_ref, ins, outs, scratch):
        total = ins[0][...].astype(f32) + ins[1][0:1]
        for r in ins[2:]:
            total = total + r[...].astype(f32)
        outs[0][...] = total.astype(bf16)

    def make_mixed(mixed_terms):
        return run(
        mixed_kernel,
        [array((block_rows, width), bf16)],
        o_grid,
        [rows_of(o_step, width), fixed(8, width)] + [rows_of(o_step, width)] * len(mixed_terms),
        [rows_of(o_step, width)],
        [tokens[0], bias_last, *mixed_terms],
        name="mixed",
    )[0]

    def tokens_kernel(at_ref, ins, outs, scratch):
        g = ins[2][...].astype(f32)
        for r in ins[3:]:
            g = g + r[...].astype(f32)
        x = ins[0][...].astype(f32)
        center = x - jnp.mean(x, axis=-1, keepdims=True)
        inv = lax.rsqrt(jnp.mean(center * center, axis=-1, keepdims=True) + norm_eps)
        n = center * inv
        inner = g - jnp.mean(g, axis=-1, keepdims=True) - n * jnp.mean(g * n, axis=-1, keepdims=True)
        outs[0][...] = ins[1][...].astype(f32) + inv * inner

    def make_grad_tokens(back_terms):
        return run(
        tokens_kernel,
        [array((block_rows, width), f32)],
        o_grid,
        [rows_of(o_step, width)] * (2 + len(back_terms)),
        [rows_of(o_step, width)],
        [tokens[0], cotangent[0], *back_terms],
        name="grad_tokens",
    )[0]
    y_d0 = rsx(down_own[0], down_got[0])
    up_sent = [grads_up(k) for k in range(1, n_y)]
    up_got = [over_y(p[0], k + 1) for k, p in enumerate(up_sent)]
    z[0] = gather_z(rsy(y_d0))
    dqkv0, qkv_sum0 = attend_back(qkv[0], do0, lse[0])
    dqkv1, qkv_sum1 = attend_back(qkv[1], do1, lse[1])
    dqkv, qkv_sums = (dqkv0, dqkv1), (qkv_sum0, qkv_sum1)
    up_own = grads_up(0)
    dots_u = [up_own[1]] + [p[1] for p in up_sent]
    y_d1 = rsx(down_own[1], down_got[1])
    mixed = make_mixed(mixed_terms)
    att_own = grads_att(0)
    up_split = split_sum([up_own[0]] + up_got, n_f, None, "sum_fsdp")
    x_u = [up_split[0]] + [over_f(up_split[k], k) for k in range(1, n_f)]
    z[1] = gather_z(rsy(y_d1))
    p0, c0, o0 = after_z(0)
    att_got, att_dots = sent([grads_att(k) for k in range(1, n_f)])
    dots_a = [att_own[-1]] + att_dots
    def norm_grads(dots, gain, shift):
        ordered = dots[0] if n_f == 1 else None
        if n_f == 2:
            pair = jnp.stack([d[:, :2] for d in dots])
            ordered = jnp.stack([jnp.where(f_idx == m, pair[0], pair[1]) for m in range(2)])
        elif n_f > 2:
            ordered = jnp.roll(jnp.stack([d[:, :2] for d in dots]), f_idx, axis=0)
        ordered = ordered.reshape(width, -1)
        return (ordered[:, 0] - shift * ordered[:, 1]) / gain, ordered[:, 1]

    g_gain1, g_shift1 = norm_grads(dots_a, gain1, shift1)
    def by_rows(dots):
        cut = [d[:, :2].reshape(n_f, y_rows, 2) for d in dots]
        parts = [
            functools.reduce(lambda so_far, k: jnp.where(jnp.mod(m - y_idx, n_y) == k, cut[k], so_far), range(1, n_y), cut[0])
            for m in range(n_y)
        ]
        return list(jnp.stack(parts, axis=1).reshape(n_f, rows, 2))

    g_gain2, g_shift2 = norm_grads(by_rows(dots_u), gain2, shift2)
    qkv_sum = qkv_sum0[0] + qkv_sum1[0]
    up_sum = up_sum0[0] + up_sum1[0]

    def spot(vec, size):
        return lax.dynamic_update_slice_in_dim(jnp.zeros((size,), f32), vec, j_idx * vec.shape[0], axis=0)

    sums = [
        g_gain1,
        g_shift1,
        g_gain2,
        g_shift2,
        spot(qkv_sum[:n_att], width),
        spot(qkv_sum[n_att : n_att + ROT], heads * ROT),
        spot(qkv_sum[2 * n_att :], width),
        jnp.sum(cotangent[0].astype(f32), axis=0),
        spot(up_sum, hidden),
    ]
    vec = jnp.concatenate(sums).reshape(-1, LANES)

    vec = pin(vec)
    place_own(0, p0, c0)
    back_other = core_swap(back(dqkv[1], pre[1]))
    p1, c1, o1 = after_z(1)
    o0 = after_y(o0)
    z[2] = gather_z(rsy(x_u))
    place_own(1, p1, c1)
    place_over(0, o0)
    back_own = back(dqkv[0], pre[0])
    vec_f = [vec] + [over_f(vec, k) for k in range(1, n_f)]
    y_a = rsx(att_own[0], att_got[0])
    o1 = after_y(o1)
    vec = add(vec_f, f32, "sum_small")
    vec_c = [vec, core_swap(vec)]
    vec = add(vec_c, f32, "sum_small")
    vec_y = [vec] + [over_y(vec, k) for k in range(1, n_y)]
    vec = add(vec_y, f32, "sum_small")
    qkv_piece, o_piece = rsy_cut(y_a, n_att)
    z[3] = gather_z(qkv_piece)
    z[4] = gather_z(stack([o_piece] + [over_y(o_piece, k) for k in range(1, n_y)]))
    p2, c2, o2 = after_z(2)
    place_own(2, p2, c2)
    place_over(1, o1)
    back_terms = [to_owners(back_own, back_other, "sum_back")]
    o2 = after_y(o2)
    p3, c3, o3 = after_z(3)
    vec_z = [vec, lax.ppermute(vec, "ctx", [(0, 1), (1, 0), (2, 3), (3, 2)])]
    place_own(3, p3, c3)
    place_over(2, o2)
    vec = add(vec_z, f32, "sum_small")
    p4, c4, _ = after_z(4, False)
    vec_z = [vec, lax.ppermute(vec, "ctx", [(0, 2), (2, 0), (1, 3), (3, 1)])]
    place_own(4, p4, c4)
    vec = add(vec_z, f32, "sum_small").reshape(-1)
    outs = []
    start = 0
    for s in sums:
        size = s.shape[0] // n_f
        outs.append(lax.dynamic_slice_in_dim(vec, start + f_idx * size, size, axis=0))
        start += s.shape[0]
    s_g1, s_b1, s_g2, s_b2, s_q, s_k, s_v, s_last, s_u = outs

    o3 = after_y(o3, outs)
    for k, (piece, _) in enumerate(o3):
        place(piece, k + 1, False, targets[3])
    grad_tokens = make_grad_tokens(back_terms)
    for k, (_, crossed) in enumerate(o3):
        place(crossed, k + 1, True, targets[3])

    return (
        mixed[None],
        grad_tokens[None],
        s_g1,
        s_b1,
        s_g2,
        s_b2,
        bufs["q"],
        bufs["k"],
        bufs["v"],
        s_q,
        s_k,
        s_v,
        bufs["o"],
        s_last,
        bufs["u"],
        s_u,
        bufs["d"],
        s_last,
    )


def solution(mesh):
    seq = P(("dp", "fsdp"), "ctx", None)
    vec, mat = P("fsdp"), P("fsdp", None)
    params_in = (vec,) * 4 + (mat,) * 3 + (vec,) * 3 + (mat, vec, mat, vec, mat, vec)
    return jax.shard_map(
        functools.partial(local, mesh.shape["dp"], mesh.shape["ctx"], mesh.shape["fsdp"]),
        mesh=mesh,
        in_specs=(seq, seq) + params_in,
        out_specs=(seq, seq) + params_in,
        check_vma=False,
    )
```
